32 devices in a mesh: ctx: 8 (over z, y), head: 4 (over x, core).
Axes of the slice: x: 2, y: 2, z: 4, core: 2. Of those that a mesh axis runs over, the one named last changes fastest.
Arguments:
- layer_input: bfloat16 [2048, 16384], P('ctx'), may hold values from -6 to 6
- queries: bfloat16 [2048, 8192], P('ctx', 'head'), may hold values from -80 to 80
- saved_keys: bfloat16 [2048, 512], P('ctx', 'head'), may hold values from -6 to 6
- saved_values: bfloat16 [2048, 512], P('ctx', 'head'), may hold values from -6 to 6
- grad_output: bfloat16 [2048, 8192], P('ctx', 'head'), may hold values from -6 to 6
- key_weight: bfloat16 [16384, 512], P(None, 'head'), may hold values from -0.25 to 0.25
- value_weight: bfloat16 [16384, 512], P(None, 'head'), may hold values from -0.25 to 0.25
- block_table: int32 [8, 2], replicated, may hold values from 0 to 15, as said below
Outputs:
- grad_queries: bfloat16 [2048, 8192], P('ctx', 'head')
- grad_key_weight: float32 [16384, 512], P('ctx', 'head')
- grad_value_weight: float32 [16384, 512], P('ctx', 'head')
- grad_input: bfloat16 [2048, 16384], P('ctx', 'head')
The draws below stay inside these ranges and needn't reach their ends.
Inputs may be any that keep to these rules, and one draw needn't show every extreme that they name: `block_table`: row r holds a block b and its mirror 2 * 8 - 1 - b, in either order; every block of 0 to 15 appears exactly once.
All inputs are finite; a program needn't handle non-finite values.
Results may differ from the reference program's by a relative error of at most 0.02.
Values may be sent and summed in bfloat16 or wider, within the bound.
A program may use at most 128 MiB of HBM per device.

```python
import jax
import jax.numpy as jnp
from jax import lax

D = 16384
HD = 128
GRP = 16
BLK = 128
KVH = 4
HQ = 64
SEQ = 2048
N_CTX = 8


def pair_table(base):
    mirror = jax.random.permutation(jax.random.fold_in(base, 11), N_CTX).astype(jnp.int32)
    flips = jax.random.randint(jax.random.fold_in(base, 12), (N_CTX,), 0, 2).astype(jnp.int32)
    other = 2 * N_CTX - 1 - mirror
    first_block = jnp.where(flips == 1, other, mirror)
    second_block = jnp.where(flips == 1, mirror, other)
    return jnp.stack([first_block, second_block], axis=1).astype(jnp.int32)


def draw_block_table(key, part):
    return pair_table(key)


def draw_saved_keys(key, part):
    values_drawn = jnp.clip(jax.random.normal(jax.random.fold_in(key, 21), (SEQ, KVH * HD), jnp.float32), -6.0, 6.0)
    return values_drawn.astype(jnp.bfloat16)


def draw_queries(key, part):
    values_drawn = jnp.clip(jax.random.normal(jax.random.fold_in(key, 22), (SEQ, HQ * HD), jnp.float32), -6.0, 6.0)
    return values_drawn.astype(jnp.bfloat16)


def with_spikes(result, rng, source, target, blocks, factor):
    owner, partner = [(jnp.arange(result.shape[axis_at]) // (result.shape[axis_at] // blocks)).reshape([-1 if axis == axis_at else 1 for axis in range(result.ndim)]) for axis_at in (source, target)]
    chosen = jax.random.permutation(rng, blocks)[partner]
    strong = (owner == chosen) | (owner == (partner + blocks // 2) % blocks)
    return jnp.where(strong, factor * result, result)


def block_scale(key, extent, shards, smallest, high):
    gain, own = 1.0, jax.random.fold_in(key, 6)
    for axis_at, blocks in shards:
        steps = jnp.exp(jax.random.uniform(jax.random.fold_in(own, axis_at), (blocks,), jnp.float32, smallest / len(shards), high / len(shards)))
        gain = gain * jnp.repeat(steps, extent[axis_at] // blocks).reshape([-1 if axis == axis_at else 1 for axis in range(len(extent))])
    return gain


def gaussian(own_key, extent, spread, reach, pieces=(), kind=jnp.bfloat16):
    result = spread * jax.random.normal(own_key, extent, jnp.float32)
    if pieces:
        result = result * block_scale(own_key, extent, pieces, -0.22, 0.18)
    return jnp.clip(result, -reach, reach).astype(kind)


def heavy_noise(rng, dims, width, limit, shards, heavy, held_as=jnp.bfloat16):
    array = width * jax.random.normal(rng, dims, jnp.float32)
    if shards:
        array = array * block_scale(rng, dims, shards, -0.22, 0.18)
    return jnp.clip(with_spikes(array, jax.random.fold_in(rng, 3), *heavy), -limit, limit).astype(held_as)


def setup_inputs(seed: int = 0) -> dict:
    streams_of = jax.random.split(jax.random.key(seed), 9)
    return {
        "layer_input": heavy_noise(streams_of[0], (SEQ, D), 1.0, 6.0, ((0, 8),), (0, 1, 8, 2.0)),
        "queries": draw_queries(jax.random.fold_in(streams_of[8], 71), 0),
        "saved_keys": draw_saved_keys(jax.random.fold_in(streams_of[8], 71), 0),
        "saved_values": gaussian(streams_of[3], (SEQ, KVH * HD), 1.0, 6.0, ((0, 8), (1, 4))),
        "grad_output": gaussian(streams_of[4], (SEQ, HQ * HD), 1.0, 6.0, ((0, 8), (1, 4))),
        "key_weight": gaussian(streams_of[5], (D, KVH * HD), (KVH * HD) ** -0.5, 0.25, ((1, 4),)),
        "value_weight": gaussian(streams_of[6], (D, KVH * HD), (KVH * HD) ** -0.5, 0.25, ((1, 4),)),
        "block_table": draw_block_table(jax.random.fold_in(streams_of[8], 71), 0),
    }


def reference(layer_input, queries, saved_keys, saved_values, grad_output, key_weight, value_weight, block_table):
    score_scale = HD ** -0.5
    block_list = block_table.reshape(-1).astype(jnp.int32)
    row_ids = jnp.arange(SEQ, dtype=jnp.int32)
    position = block_list[row_ids // BLK] * BLK + row_ids % BLK
    causal = position[None, :] <= position[:, None]
    query_heads = queries.reshape(SEQ, KVH, GRP, HD).transpose(1, 2, 0, 3)
    output_heads = grad_output.reshape(SEQ, KVH, GRP, HD).transpose(1, 2, 0, 3)
    key_heads = saved_keys.reshape(SEQ, KVH, HD).transpose(1, 0, 2)
    value_heads = saved_values.reshape(SEQ, KVH, HD).transpose(1, 0, 2)

    def one_head(head_queries, head_keys, head_values, head_grads):
        logits = jnp.dot(head_queries, head_keys.T, preferred_element_type=jnp.float32) * score_scale
        logits = jnp.where(causal, logits, -jnp.inf)
        row_top = jnp.max(logits, axis=-1, keepdims=True)
        log_norm = row_top + jnp.log(jnp.sum(jnp.exp(logits - row_top), axis=-1, keepdims=True))
        probability = jnp.exp(logits - log_norm)
        grad_probs = jnp.dot(head_grads, head_values.T, preferred_element_type=jnp.float32)
        row_delta = jnp.sum(probability * grad_probs, axis=-1, keepdims=True)
        grad_logits = (probability * (grad_probs - row_delta)).astype(jnp.bfloat16)
        grad_query = jnp.dot(grad_logits, head_keys, preferred_element_type=jnp.float32) * score_scale
        grad_key = jnp.dot(grad_logits.T, head_queries, preferred_element_type=jnp.float32) * score_scale
        grad_value = jnp.dot(probability.astype(jnp.bfloat16).T, head_grads, preferred_element_type=jnp.float32)
        return grad_query.astype(jnp.bfloat16), grad_key, grad_value

    def group_grads(inputs):
        group_queries, group_keys, group_values, group_outputs = inputs

        def advance(state, head_inputs):
            grad_query, grad_key, grad_value = one_head(head_inputs[0], group_keys, group_values, head_inputs[1])
            return (state[0] + grad_key, state[1] + grad_value), grad_query

        zeros_kv = jnp.zeros((SEQ, HD), jnp.float32)
        sums, grad_query = lax.scan(advance, (zeros_kv, zeros_kv), (group_queries, group_outputs))
        return grad_query, sums[0].astype(jnp.bfloat16), sums[1].astype(jnp.bfloat16)

    grad_query, key_grads, value_grads = lax.map(group_grads, (query_heads, key_heads, value_heads, output_heads))
    grad_queries = grad_query.transpose(2, 0, 1, 3).reshape(SEQ, HQ * HD)
    key_all = key_grads.transpose(1, 0, 2).reshape(SEQ, KVH * HD)
    value_all = value_grads.transpose(1, 0, 2).reshape(SEQ, KVH * HD)
    grad_key_weight = jnp.dot(layer_input.T, key_all, preferred_element_type=jnp.float32)
    grad_value_weight = jnp.dot(layer_input.T, value_all, preferred_element_type=jnp.float32)
    key_mats = key_weight.reshape(D, KVH, HD).transpose(1, 0, 2)
    value_mats = value_weight.reshape(D, KVH, HD).transpose(1, 0, 2)

    def add_head(total, head_inputs):
        head_key_grad, head_value_grad, head_key_mat, head_value_mat = head_inputs
        input_term = jnp.dot(head_key_grad, head_key_mat.T, preferred_element_type=jnp.float32)
        input_term = input_term + jnp.dot(head_value_grad, head_value_mat.T, preferred_element_type=jnp.float32)
        rounded = lax.optimization_barrier(input_term.astype(jnp.bfloat16))
        return total + rounded.astype(jnp.float32), None

    total, unused = lax.scan(add_head, jnp.zeros((SEQ, D), jnp.float32), (key_grads, value_grads, key_mats, value_mats))
    return grad_queries, grad_key_weight, grad_value_weight, total.astype(jnp.bfloat16)
```

```python
import functools
import math

import jax
import jax.numpy as jnp
from jax import lax
from jax.experimental import pallas as pl
from jax.experimental.pallas import tpu as pltpu
from jax.sharding import PartitionSpec as P

HD = 128
MESH = pl.DeviceIdType.MESH
NT = (((1,), (1,)), ((), ()))
NN = (((1,), (0,)), ((), ()))


def kernel(
    n_ctx,
    n_head,
    table,
    inverse,
    q_ref,
    g_ref,
    kv_ref,
    x_ref,
    kw_ref,
    vw_ref,
    dq_ref,
    x_all,
    w_all,
    rows_all,
    rows_heads,
    kv_all,
    keys,
    values,
    keys_t,
    scores,
    dprobs,
    acc_k,
    acc_v,
    part,
    received,
    own_rows,
    gather_send,
    gather_recv,
    x_send,
    x_recv,
    pair_send,
    pair_recv,
    w_send,
    w_recv,
    sum_send,
    sum_recv,
    rows_send,
    rows_recv,
    heads_send,
    heads_recv,
    local_sem,
):
    me = lax.axis_index("ctx")
    head = lax.axis_index("head")
    core = lax.rem(head, 2)
    partner = head + 1 - 2 * core
    tokens = q_ref.shape[0]
    blk = tokens // 2
    heads = q_ref.shape[1] // HD
    seq = tokens * n_ctx
    blocks = 2 * n_ctx
    cols = x_ref.shape[1] // n_ctx
    half = cols // 2
    feats = kw_ref.shape[0] // n_head
    scale = HD**-0.5
    log2_scale = scale * math.log2(math.e)

    def ctx_peer(d):
        return lax.rem(me + d, n_ctx)

    def ctx_source(d):
        return lax.rem(me + n_ctx - d, n_ctx)

    def head_peer(d):
        return lax.rem(head + d, n_head)

    def ctx_copy(src, dst, send, recv, d):
        return pltpu.make_async_remote_copy(
            src_ref=src,
            dst_ref=dst,
            send_sem=send.at[d],
            recv_sem=recv.at[d],
            device_id=(ctx_peer(d), head),
            device_id_type=MESH,
        )

    def head_copy(src, dst, send, recv, at, to):
        return pltpu.make_async_remote_copy(
            src_ref=src,
            dst_ref=dst,
            send_sem=send.at[at],
            recv_sem=recv.at[at],
            device_id=(me, to),
            device_id_type=MESH,
        )

    barrier = pltpu.get_barrier_semaphore()
    for d in range(1, n_ctx):
        pl.semaphore_signal(barrier, inc=1, device_id=(ctx_peer(d), head), device_id_type=MESH)
    for d in range(1, n_head):
        pl.semaphore_signal(barrier, inc=1, device_id=(me, head_peer(d)), device_id_type=MESH)
    pl.semaphore_wait(barrier, n_ctx + n_head - 2)

    own = pl.ds(pl.multiple_of(me * tokens, tokens), tokens)
    gathers = [
        ctx_copy(kv_ref, kv_all.at[pl.ds(2 * me, 2)], gather_send, gather_recv, d) for d in range(1, n_ctx)
    ]
    for copy in gathers:
        copy.start()
    locals_ = [
        pltpu.make_async_copy(
            x_ref.at[:, pl.ds(pl.multiple_of(me * cols, cols), cols)],
            x_all.at[own],
            local_sem.at[0],
        )
    ]
    own_feats = pl.ds(pl.multiple_of(head * feats, feats), feats)
    for i, ref in enumerate((kw_ref, vw_ref)):
        locals_.append(
            pltpu.make_async_copy(
                ref.at[own_feats],
                w_all.at[:, pl.ds(pl.multiple_of((head * 2 + i) * HD, HD), HD)],
                local_sem.at[1 + i],
            )
        )
    for copy in locals_:
        copy.start()
    kv_all[pl.ds(2 * me, 2)] = kv_ref[...]
    for copy in gathers:
        copy.wait()

    x_copies = []
    for d in range(1, n_ctx):
        first = ctx_peer(d) * cols + core * half
        x_copies.append(
            ctx_copy(
                x_ref.at[:, pl.ds(pl.multiple_of(first, half), half)],
                x_all.at[own, pl.ds(pl.multiple_of(core * half, half), half)],
                x_send,
                x_recv,
                d,
            )
        )
    w_copies = []
    for d in range(1, n_head):
        to = head_peer(d)
        for i, ref in enumerate((kw_ref, vw_ref)):
            w_copies.append(
                head_copy(
                    ref.at[pl.ds(pl.multiple_of(to * feats, feats), feats)],
                    w_all.at[:, pl.ds(pl.multiple_of((head * 2 + i) * HD, HD), HD)],
                    w_send,
                    w_recv,
                    2 * d + i,
                    to,
                )
            )
    for copy in x_copies + w_copies:
        copy.start()

    def sort_block(u, carry):
        from_rows = kv_all[inverse[u]]
        to_rows = pl.ds(pl.multiple_of(u * blk, blk), blk)
        keys[to_rows, :] = from_rows[:, :HD]
        values[to_rows, :] = from_rows[:, HD:]
        keys_t[:, to_rows] = from_rows[:, :HD].T
        return carry

    lax.fori_loop(0, blocks, sort_block, 0)
    acc_k[...] = jnp.zeros_like(acc_k)
    acc_v[...] = jnp.zeros_like(acc_v)

    block_0 = table[2 * me]
    block_1 = table[2 * me + 1]
    top_block = jnp.maximum(block_0, block_1)
    chunk = min(512, seq // 2)
    width = 2 * blk

    first_is_top = jnp.full((width, HD), block_0, jnp.int32) == top_block

    def load(ref, pair):
        halves = []
        for slot in range(2):
            rows = slice(slot * blk, (slot + 1) * blk)
            halves.append(
                jnp.concatenate(
                    [
                        ref[rows, pl.ds(pl.multiple_of((2 * pair + i) * HD, HD), HD)]
                        for i in range(2)
                    ],
                    axis=0,
                ).astype(jnp.float32)
            )
        first, second = halves
        return (
            jnp.where(first_is_top, first, second).astype(jnp.bfloat16),
            jnp.where(first_is_top, second, first).astype(jnp.bfloat16),
        )

    def attend(q, g, block_id, extent, free):
        top = None
        for start in range(0, extent, chunk):
            rows = slice(start, start + chunk)
            s = lax.dot_general(keys[rows, :], q, NT, preferred_element_type=jnp.float32)
            if start + chunk > free:
                key_pos = lax.broadcasted_iota(jnp.int32, (chunk, width), 0)
                row_pos = lax.rem(lax.broadcasted_iota(jnp.int32, (chunk, width), 1), blk)
                s = jnp.where(key_pos - row_pos <= block_id * blk - start, s, -1e30)
            scores[rows, :] = s
            here = jnp.max(s, axis=0, keepdims=True)
            top = here if top is None else jnp.maximum(top, here)
        top = top * log2_scale
        norm = jnp.zeros((1, width), jnp.float32)
        delta = jnp.zeros((1, width), jnp.float32)
        for start in range(0, extent, chunk):
            rows = slice(start, start + chunk)
            prob = jnp.exp2(scores[rows, :] * log2_scale - top)
            dp = lax.dot_general(values[rows, :], g, NT, preferred_element_type=jnp.float32)
            norm = norm + jnp.sum(prob, axis=0, keepdims=True)
            delta = delta + jnp.sum(prob * dp, axis=0, keepdims=True)
            scores[rows, :] = prob
            dprobs[rows, :] = dp
        inv = 1.0 / norm
        delta = delta * inv
        dq_t = jnp.zeros((HD, width), jnp.float32)
        for start in range(0, extent, chunk):
            rows = slice(start, start + chunk)
            prob = scores[rows, :] * inv
            ds = (prob * (dprobs[rows, :] - delta)).astype(jnp.bfloat16)
            pieces = slice(start // blk, (start + chunk) // blk)
            acc_v[pieces] += lax.dot_general(
                prob.astype(jnp.bfloat16), g, NN, preferred_element_type=jnp.float32
            ).reshape(-1, blk, HD)
            acc_k[pieces] += lax.dot_general(
                ds, q, NN, preferred_element_type=jnp.float32
            ).reshape(-1, blk, HD)
            dq_t = dq_t + lax.dot_general(
                keys_t[:, rows], ds, NN, preferred_element_type=jnp.float32
            )
        return jnp.concatenate(
            [dq_t[:, i * blk : (i + 1) * blk].T for i in range(2)], axis=0
        ) * scale

    def head_pair(pair, carry):
        q_top, q_low = load(q_ref, pair)
        g_top, g_low = load(g_ref, pair)
        top_grad = attend(q_top, g_top, top_block, seq, seq // 2)
        low_grad = attend(q_low, g_low, blocks - 1 - top_block, seq // 2, 0)
        for slot, grads in enumerate(
            (
                jnp.where(first_is_top, top_grad, low_grad),
                jnp.where(first_is_top, low_grad, top_grad),
            )
        ):
            for i in range(2):
                dq_ref[
                    slot * blk : (slot + 1) * blk,
                    pl.ds(pl.multiple_of((2 * pair + i) * HD, HD), HD),
                ] = grads[i * blk : (i + 1) * blk].astype(jnp.bfloat16)
        return carry

    lax.fori_loop(0, heads // 2, head_pair, 0)

    def unsort(s, carry):
        to_rows = pl.ds(pl.multiple_of(s * blk, blk), blk)
        part[to_rows, :HD] = (acc_k[table[s]] * scale).astype(jnp.bfloat16)
        part[to_rows, HD:] = acc_v[table[s]].astype(jnp.bfloat16)
        return carry

    lax.fori_loop(0, blocks, unsort, 0)

    sums = []
    for d in range(1, n_ctx):
        to_rows = pl.ds(pl.multiple_of(ctx_peer(d) * tokens, tokens), tokens)
        sums.append(ctx_copy(part.at[to_rows], received.at[d], sum_send, sum_recv, d))
    for copy in sums:
        copy.start()
    for copy in sums:
        copy.wait()
    total = part[own, :].astype(jnp.float32)
    for d in range(1, n_ctx):
        total = total + received[d].astype(jnp.float32)
    own_rows[...] = total.astype(jnp.bfloat16)

    head_cols = pl.ds(pl.multiple_of(head * 2 * HD, 2 * HD), 2 * HD)
    locals_.append(pltpu.make_async_copy(own_rows, rows_all.at[own], local_sem.at[3]))
    locals_.append(pltpu.make_async_copy(own_rows, rows_heads.at[:, head_cols], local_sem.at[4]))
    for copy in locals_[3:]:
        copy.start()
    rows_copies = [
        ctx_copy(own_rows, rows_all.at[own], rows_send, rows_recv, d) for d in range(1, n_ctx)
    ]
    for d in range(1, n_head):
        rows_copies.append(
            head_copy(
                own_rows, rows_heads.at[:, head_cols], heads_send, heads_recv, d, head_peer(d)
            )
        )
    for copy in rows_copies:
        copy.start()

    pair_copies = []
    for d in range(1, n_ctx):
        x_copies[d - 1].wait()
        source = ctx_source(d)
        piece = x_all.at[
            pl.ds(pl.multiple_of(source * tokens, tokens), tokens),
            pl.ds(pl.multiple_of(core * half, half), half),
        ]
        copy = head_copy(piece, piece, pair_send, pair_recv, d, partner)
        copy.start()
        pair_copies.append(copy)
    for copy in w_copies + rows_copies + pair_copies + locals_:
        copy.wait()


def local(
    n_ctx,
    n_head,
    layer_input,
    queries,
    saved_keys,
    saved_values,
    grad_output,
    key_weight,
    value_weight,
    block_table,
):
    tokens = queries.shape[0]
    blk = tokens // 2
    seq = tokens * n_ctx
    cols = layer_input.shape[1] // n_ctx
    feats = key_weight.shape[0] // n_head
    table = block_table.reshape(-1)
    slots = jnp.arange(table.shape[0], dtype=jnp.int32)
    inverse = jnp.sum(jnp.where(table[None, :] == slots[:, None], slots[None, :], 0), axis=1)
    saved = jnp.concatenate([saved_keys, saved_values], axis=1).reshape(2, blk, 2 * HD)
    smem = pl.BlockSpec(memory_space=pltpu.SMEM)
    vmem = pl.BlockSpec(memory_space=pltpu.VMEM)
    hbm = pl.BlockSpec(memory_space=pl.ANY)
    bf16 = jnp.bfloat16
    f32 = jnp.float32
    dma = pltpu.SemaphoreType.DMA
    dq, x_all, w_all, rows_all, rows_heads = pl.pallas_call(
        functools.partial(kernel, n_ctx, n_head),
        out_shape=(
            jax.ShapeDtypeStruct(queries.shape, bf16),
            jax.ShapeDtypeStruct((seq, cols), bf16),
            jax.ShapeDtypeStruct((feats, n_head * 2 * HD), bf16),
            jax.ShapeDtypeStruct((seq, 2 * HD), bf16),
            jax.ShapeDtypeStruct((tokens, n_head * 2 * HD), bf16),
        ),
        in_specs=[smem, smem, vmem, vmem, vmem, hbm, hbm, hbm],
        out_specs=(vmem, hbm, hbm, hbm, hbm),
        scratch_shapes=[
            pltpu.VMEM((2 * n_ctx, blk, 2 * HD), bf16),
            pltpu.VMEM((seq, HD), bf16),
            pltpu.VMEM((seq, HD), bf16),
            pltpu.VMEM((HD, seq), bf16),
            pltpu.VMEM((seq, 2 * blk), f32),
            pltpu.VMEM((seq, 2 * blk), f32),
            pltpu.VMEM((2 * n_ctx, blk, HD), f32),
            pltpu.VMEM((2 * n_ctx, blk, HD), f32),
            pltpu.VMEM((seq, 2 * HD), bf16),
            pltpu.VMEM((n_ctx, tokens, 2 * HD), bf16),
            pltpu.VMEM((tokens, 2 * HD), bf16),
            dma((n_ctx,)),
            dma((n_ctx,)),
            dma((n_ctx,)),
            dma((n_ctx,)),
            dma((n_ctx,)),
            dma((n_ctx,)),
            dma((2 * n_head,)),
            dma((2 * n_head,)),
            dma((n_ctx,)),
            dma((n_ctx,)),
            dma((n_ctx,)),
            dma((n_ctx,)),
            dma((n_head,)),
            dma((n_head,)),
            dma((5,)),
        ],
        compiler_params=pltpu.CompilerParams(
            collective_id=0, has_side_effects=True, vmem_limit_bytes=48 * 1024 * 1024
        ),
    )(table, inverse, queries, grad_output, saved, layer_input, key_weight, value_weight)
    contract = (((0,), (0,)), ((), ()))
    gradients = lax.dot_general(x_all, rows_all, contract, preferred_element_type=f32)
    grad_input = lax.dot_general(rows_heads, w_all, NT, preferred_element_type=f32).astype(bf16)
    return dq, gradients[:, :HD], gradients[:, HD:], grad_input


def solution(mesh):
    both = P("ctx", "head")
    in_specs = (P("ctx", None), both, both, both, both, P(None, "head"), P(None, "head"), P())
    out_specs = (both, both, both, both)
    return jax.shard_map(
        functools.partial(local, mesh.shape["ctx"], mesh.shape["head"]),
        mesh=mesh,
        in_specs=in_specs,
        out_specs=out_specs,
        check_vma=False,
    )
```

```python
import functools
import math

import jax
import jax.numpy as jnp
from jax import lax
from jax.experimental import pallas as pl
from jax.experimental.pallas import tpu as pltpu
from jax.sharding import PartitionSpec as P

HD = 128
MESH = pl.DeviceIdType.MESH
NT = (((1,), (1,)), ((), ()))
NN = (((1,), (0,)), ((), ()))


def kernel(
    n_ctx,
    n_head,
    table,
    inverse,
    q_ref,
    g_ref,
    kv_ref,
    x_ref,
    kw_ref,
    vw_ref,
    dq_ref,
    x_all,
    w_all,
    rows_all,
    rows_heads,
    kv_all,
    keys,
    values,
    keys_t,
    scores,
    dprobs,
    acc_k,
    acc_v,
    part,
    received,
    own_rows,
    paired,
    outgoing,
    gather_send,
    gather_recv,
    gather_pair_send,
    gather_pair_recv,
    side_send,
    side_recv,
    side_pair_send,
    side_pair_recv,
    x_send,
    x_recv,
    pair_send,
    pair_recv,
    w_send,
    w_recv,
    sum_send,
    sum_recv,
    sum_pair_send,
    sum_pair_recv,
    rows_send,
    rows_recv,
    rows_pair_send,
    rows_pair_recv,
    heads_send,
    heads_recv,
    local_sem,
):
    me = lax.axis_index("ctx")
    head = lax.axis_index("head")
    core = lax.rem(head, 2)
    partner = head + 1 - 2 * core
    side = lax.rem(head // 2, 2)
    across = head + 2 - 4 * side
    ctx_partner = me + 1 - 2 * lax.rem(me, 2)
    strides = n_ctx // 2
    tokens = q_ref.shape[0]
    blk = tokens // 2
    heads = q_ref.shape[1] // HD
    seq = tokens * n_ctx
    blocks = 2 * n_ctx
    cols = x_ref.shape[1] // n_ctx
    half = cols // 2
    feats = kw_ref.shape[0] // n_head
    scale = HD**-0.5
    log2_scale = scale * math.log2(math.e)

    def ctx_peer(d):
        return lax.rem(me + d, n_ctx)

    def ctx_source(d):
        return lax.rem(me + n_ctx - d, n_ctx)

    def head_peer(d):
        return lax.rem(head + d, n_head)

    def ctx_copy(src, dst, send, recv, at, to):
        return pltpu.make_async_remote_copy(
            src_ref=src,
            dst_ref=dst,
            send_sem=send.at[at],
            recv_sem=recv.at[at],
            device_id=(to, head),
            device_id_type=MESH,
        )

    def gather(src, place, sems):
        direct = [
            ctx_copy(src, place(me), sems[0], sems[1], k, ctx_peer(2 * k))
            for k in range(1, strides)
        ]
        passed = [ctx_copy(src, place(me), sems[2], sems[3], 0, ctx_partner)]
        for copy in direct + passed:
            copy.start()
        return direct, passed

    def gather_on(direct, passed, place, sems):
        for k in range(1, strides):
            direct[k - 1].wait()
            piece = place(ctx_source(2 * k))
            copy = ctx_copy(piece, piece, sems[2], sems[3], k, ctx_partner)
            copy.start()
            passed.append(copy)
        for copy in passed:
            copy.wait()

    def head_copy(src, dst, send, recv, at, to):
        return pltpu.make_async_remote_copy(
            src_ref=src,
            dst_ref=dst,
            send_sem=send.at[at],
            recv_sem=recv.at[at],
            device_id=(me, to),
            device_id_type=MESH,
        )

    barrier = pltpu.get_barrier_semaphore()
    for d in range(1, n_ctx):
        pl.semaphore_signal(barrier, inc=1, device_id=(ctx_peer(d), head), device_id_type=MESH)
    for d in range(1, n_head):
        pl.semaphore_signal(barrier, inc=1, device_id=(me, head_peer(d)), device_id_type=MESH)
    pl.semaphore_wait(barrier, n_ctx + n_head - 2)

    own = pl.ds(pl.multiple_of(me * tokens, tokens), tokens)
    def kv_place(source):
        return kv_all.at[pl.ds(2 * source, 2)]

    kv_sems = (gather_send, gather_recv, gather_pair_send, gather_pair_recv)
    kv_direct, kv_passed = gather(kv_ref, kv_place, kv_sems)
    w_copies = []
    for d in range(1, n_head):
        to = head_peer(d)
        for i, ref in enumerate((kw_ref, vw_ref)):
            w_copies.append(
                head_copy(
                    ref.at[pl.ds(pl.multiple_of(to * feats, feats), feats)],
                    w_all.at[:, pl.ds(pl.multiple_of((head * 2 + i) * HD, HD), HD)],
                    w_send,
                    w_recv,
                    2 * d + i,
                    to,
                )
            )
    for copy in w_copies:
        copy.start()
    locals_ = [
        pltpu.make_async_copy(
            x_ref.at[:, pl.ds(pl.multiple_of(me * cols, cols), cols)],
            x_all.at[own],
            local_sem.at[0],
        )
    ]
    own_feats = pl.ds(pl.multiple_of(head * feats, feats), feats)
    for i, ref in enumerate((kw_ref, vw_ref)):
        locals_.append(
            pltpu.make_async_copy(
                ref.at[own_feats],
                w_all.at[:, pl.ds(pl.multiple_of((head * 2 + i) * HD, HD), HD)],
                local_sem.at[1 + i],
            )
        )
    for copy in locals_:
        copy.start()
    kv_all[pl.ds(2 * me, 2)] = kv_ref[...]
    gather_on(kv_direct, kv_passed, kv_place, kv_sems)

    quarter = half // 4
    direct_first = core * half + side * quarter
    x_copies = []
    for d in range(1, n_ctx):
        first = ctx_peer(d) * cols + direct_first
        x_copies.append(
            ctx_copy(
                x_ref.at[:, pl.ds(pl.multiple_of(first, quarter), half - quarter)],
                x_all.at[own, pl.ds(pl.multiple_of(direct_first, quarter), half - quarter)],
                x_send,
                x_recv,
                d,
                ctx_peer(d),
            )
        )
    for copy in x_copies:
        copy.start()

    def sort_block(u, carry):
        from_rows = kv_all[inverse[u]]
        to_rows = pl.ds(pl.multiple_of(u * blk, blk), blk)
        keys[to_rows, :] = from_rows[:, :HD]
        values[to_rows, :] = from_rows[:, HD:]
        keys_t[:, to_rows] = from_rows[:, :HD].T
        return carry

    lax.fori_loop(0, blocks, sort_block, 0)
    acc_k[...] = jnp.zeros_like(acc_k)
    acc_v[...] = jnp.zeros_like(acc_v)

    block_0 = table[2 * me]
    block_1 = table[2 * me + 1]
    top_block = jnp.maximum(block_0, block_1)
    chunk = min(512, seq // 2)
    width = 2 * blk

    first_is_top = jnp.full((width, HD), block_0, jnp.int32) == top_block

    def load(ref, pair):
        halves = []
        for slot in range(2):
            rows = slice(slot * blk, (slot + 1) * blk)
            halves.append(
                jnp.concatenate(
                    [
                        ref[rows, pl.ds(pl.multiple_of((2 * pair + i) * HD, HD), HD)]
                        for i in range(2)
                    ],
                    axis=0,
                ).astype(jnp.float32)
            )
        first, second = halves
        return (
            jnp.where(first_is_top, first, second).astype(jnp.bfloat16),
            jnp.where(first_is_top, second, first).astype(jnp.bfloat16),
        )

    def attend(q, g, block_id, extent, free):
        top = None
        for start in range(0, extent, chunk):
            rows = slice(start, start + chunk)
            s = lax.dot_general(keys[rows, :], q, NT, preferred_element_type=jnp.float32)
            if start + chunk > free:
                key_pos = lax.broadcasted_iota(jnp.int32, (chunk, width), 0)
                row_pos = lax.rem(lax.broadcasted_iota(jnp.int32, (chunk, width), 1), blk)
                s = jnp.where(key_pos - row_pos <= block_id * blk - start, s, -1e30)
            scores[rows, :] = s
            here = jnp.max(s, axis=0, keepdims=True)
            top = here if top is None else jnp.maximum(top, here)
        top = top * log2_scale
        norm = jnp.zeros((1, width), jnp.float32)
        delta = jnp.zeros((1, width), jnp.float32)
        for start in range(0, extent, chunk):
            rows = slice(start, start + chunk)
            prob = jnp.exp2(scores[rows, :] * log2_scale - top)
            dp = lax.dot_general(values[rows, :], g, NT, preferred_element_type=jnp.float32)
            norm = norm + jnp.sum(prob, axis=0, keepdims=True)
            delta = delta + jnp.sum(prob * dp, axis=0, keepdims=True)
            scores[rows, :] = prob
            dprobs[rows, :] = dp
        inv = 1.0 / norm
        delta = delta * inv
        dq_t = jnp.zeros((HD, width), jnp.float32)
        for start in range(0, extent, chunk):
            rows = slice(start, start + chunk)
            prob = scores[rows, :] * inv
            ds = (prob * (dprobs[rows, :] - delta)).astype(jnp.bfloat16)
            pieces = slice(start // blk, (start + chunk) // blk)
            acc_v[pieces] += lax.dot_general(
                prob.astype(jnp.bfloat16), g, NN, preferred_element_type=jnp.float32
            ).reshape(-1, blk, HD)
            acc_k[pieces] += lax.dot_general(
                ds, q, NN, preferred_element_type=jnp.float32
            ).reshape(-1, blk, HD)
            dq_t = dq_t + lax.dot_general(
                keys_t[:, rows], ds, NN, preferred_element_type=jnp.float32
            )
        return jnp.concatenate(
            [dq_t[:, i * blk : (i + 1) * blk].T for i in range(2)], axis=0
        ) * scale

    def head_pair(pair, carry):
        q_top, q_low = load(q_ref, pair)
        g_top, g_low = load(g_ref, pair)
        top_grad = attend(q_top, g_top, top_block, seq, seq // 2)
        low_grad = attend(q_low, g_low, blocks - 1 - top_block, seq // 2, 0)
        for slot, grads in enumerate(
            (
                jnp.where(first_is_top, top_grad, low_grad),
                jnp.where(first_is_top, low_grad, top_grad),
            )
        ):
            for i in range(2):
                dq_ref[
                    slot * blk : (slot + 1) * blk,
                    pl.ds(pl.multiple_of((2 * pair + i) * HD, HD), HD),
                ] = grads[i * blk : (i + 1) * blk].astype(jnp.bfloat16)
        return carry

    lax.fori_loop(0, heads // 2, head_pair, 0)

    def unsort(s, carry):
        to_rows = pl.ds(pl.multiple_of(s * blk, blk), blk)
        part[to_rows, :HD] = (acc_k[table[s]] * scale).astype(jnp.bfloat16)
        part[to_rows, HD:] = acc_v[table[s]].astype(jnp.bfloat16)
        return carry

    lax.fori_loop(0, blocks, unsort, 0)

    pair_sums = []
    for k in range(strides):
        target = lax.rem(ctx_partner + 2 * k, n_ctx)
        to_rows = pl.ds(pl.multiple_of(target * tokens, tokens), tokens)
        pair_sums.append(
            ctx_copy(
                part.at[to_rows], paired.at[k], sum_pair_send, sum_pair_recv, k, ctx_partner
            )
        )
    order = list(range(1, strides)) + [0]
    for k in order:
        pair_sums[k].start()
    sums = []
    for k in order:
        pair_sums[k].wait()
        rows = pl.ds(pl.multiple_of(ctx_peer(2 * k) * tokens, tokens), tokens)
        total = part[rows, :].astype(jnp.float32) + paired[k].astype(jnp.float32)
        if k:
            outgoing[k] = total.astype(jnp.bfloat16)
            copy = ctx_copy(
                outgoing.at[k], received.at[k], sum_send, sum_recv, k, ctx_peer(2 * k)
            )
            copy.start()
            sums.append(copy)
    for k in range(1, strides):
        sums[k - 1].wait()
        total = total + received[k].astype(jnp.float32)
    own_rows[...] = total.astype(jnp.bfloat16)

    head_cols = pl.ds(pl.multiple_of(head * 2 * HD, 2 * HD), 2 * HD)
    locals_.append(pltpu.make_async_copy(own_rows, rows_all.at[own], local_sem.at[3]))
    locals_.append(pltpu.make_async_copy(own_rows, rows_heads.at[:, head_cols], local_sem.at[4]))
    for copy in locals_[3:]:
        copy.start()
    def rows_place(source):
        return rows_all.at[pl.ds(pl.multiple_of(source * tokens, tokens), tokens)]

    rows_sems = (rows_send, rows_recv, rows_pair_send, rows_pair_recv)
    rows_direct, rows_passed = gather(own_rows, rows_place, rows_sems)
    rows_copies = []
    for d in range(1, n_head):
        rows_copies.append(
            head_copy(
                own_rows, rows_heads.at[:, head_cols], heads_send, heads_recv, d, head_peer(d)
            )
        )
    for copy in rows_copies:
        copy.start()

    def x_piece(d, first, size):
        return x_all.at[
            pl.ds(pl.multiple_of(ctx_source(d) * tokens, tokens), tokens),
            pl.ds(pl.multiple_of(first, quarter), size),
        ]

    side_copies = []
    pair_copies = []
    for d in range(1, n_ctx):
        x_copies[d - 1].wait()
        edge = x_piece(d, core * half + side * 3 * quarter, quarter)
        copy = head_copy(edge, edge, side_send, side_recv, d, across)
        copy.start()
        side_copies.append(copy)
        piece = x_piece(d, direct_first, half - quarter)
        copy = head_copy(piece, piece, pair_send, pair_recv, d, partner)
        copy.start()
        pair_copies.append(copy)
    gather_on(rows_direct, rows_passed, rows_place, rows_sems)
    for d in range(1, n_ctx):
        side_copies[d - 1].wait()
        piece = x_piece(d, core * half + (1 - side) * 3 * quarter, quarter)
        copy = head_copy(piece, piece, side_pair_send, side_pair_recv, d, partner)
        copy.start()
        pair_copies.append(copy)
    for copy in w_copies + rows_copies + pair_copies + locals_:
        copy.wait()


def local(
    n_ctx,
    n_head,
    layer_input,
    queries,
    saved_keys,
    saved_values,
    grad_output,
    key_weight,
    value_weight,
    block_table,
):
    tokens = queries.shape[0]
    blk = tokens // 2
    seq = tokens * n_ctx
    cols = layer_input.shape[1] // n_ctx
    feats = key_weight.shape[0] // n_head
    table = block_table.reshape(-1)
    slots = jnp.arange(table.shape[0], dtype=jnp.int32)
    inverse = jnp.sum(jnp.where(table[None, :] == slots[:, None], slots[None, :], 0), axis=1)
    saved = jnp.concatenate([saved_keys, saved_values], axis=1).reshape(2, blk, 2 * HD)
    smem = pl.BlockSpec(memory_space=pltpu.SMEM)
    vmem = pl.BlockSpec(memory_space=pltpu.VMEM)
    hbm = pl.BlockSpec(memory_space=pl.ANY)
    bf16 = jnp.bfloat16
    f32 = jnp.float32
    dma = pltpu.SemaphoreType.DMA
    dq, x_all, w_all, rows_all, rows_heads = pl.pallas_call(
        functools.partial(kernel, n_ctx, n_head),
        out_shape=(
            jax.ShapeDtypeStruct(queries.shape, bf16),
            jax.ShapeDtypeStruct((seq, cols), bf16),
            jax.ShapeDtypeStruct((feats, n_head * 2 * HD), bf16),
            jax.ShapeDtypeStruct((seq, 2 * HD), bf16),
            jax.ShapeDtypeStruct((tokens, n_head * 2 * HD), bf16),
        ),
        in_specs=[smem, smem, vmem, vmem, vmem, hbm, hbm, hbm],
        out_specs=(vmem, hbm, hbm, hbm, hbm),
        scratch_shapes=[
            pltpu.VMEM((2 * n_ctx, blk, 2 * HD), bf16),
            pltpu.VMEM((seq, HD), bf16),
            pltpu.VMEM((seq, HD), bf16),
            pltpu.VMEM((HD, seq), bf16),
            pltpu.VMEM((seq, 2 * blk), f32),
            pltpu.VMEM((seq, 2 * blk), f32),
            pltpu.VMEM((2 * n_ctx, blk, HD), f32),
            pltpu.VMEM((2 * n_ctx, blk, HD), f32),
            pltpu.VMEM((seq, 2 * HD), bf16),
            pltpu.VMEM((n_ctx, tokens, 2 * HD), bf16),
            pltpu.VMEM((tokens, 2 * HD), bf16),
            pltpu.VMEM((n_ctx // 2, tokens, 2 * HD), bf16),
            pltpu.VMEM((n_ctx // 2, tokens, 2 * HD), bf16),
            dma((n_ctx,)),
            dma((n_ctx,)),
            dma((n_ctx,)),
            dma((n_ctx,)),
            dma((n_ctx,)),
            dma((n_ctx,)),
            dma((n_ctx,)),
            dma((n_ctx,)),
            dma((n_ctx,)),
            dma((n_ctx,)),
            dma((n_ctx,)),
            dma((n_ctx,)),
            dma((2 * n_head,)),
            dma((2 * n_head,)),
            dma((n_ctx,)),
            dma((n_ctx,)),
            dma((n_ctx,)),
            dma((n_ctx,)),
            dma((n_ctx,)),
            dma((n_ctx,)),
            dma((n_ctx,)),
            dma((n_ctx,)),
            dma((n_head,)),
            dma((n_head,)),
            dma((5,)),
        ],
        compiler_params=pltpu.CompilerParams(
            collective_id=0, has_side_effects=True, vmem_limit_bytes=48 * 1024 * 1024
        ),
    )(table, inverse, queries, grad_output, saved, layer_input, key_weight, value_weight)
    contract = (((0,), (0,)), ((), ()))
    gradients = lax.dot_general(x_all, rows_all, contract, preferred_element_type=f32)
    grad_input = lax.dot_general(rows_heads, w_all, NT, preferred_element_type=f32).astype(bf16)
    return dq, gradients[:, :HD], gradients[:, HD:], grad_input


def solution(mesh):
    both = P("ctx", "head")
    in_specs = (P("ctx", None), both, both, both, both, P(None, "head"), P(None, "head"), P())
    out_specs = (both, both, both, both)
    return jax.shard_map(
        functools.partial(local, mesh.shape["ctx"], mesh.shape["head"]),
        mesh=mesh,
        in_specs=in_specs,
        out_specs=out_specs,
        check_vma=False,
    )
```

```python
import functools
import math

import jax
import jax.numpy as jnp
from jax import lax
from jax.experimental import pallas as pl
from jax.experimental.pallas import tpu as pltpu
from jax.sharding import PartitionSpec as P

HD = 128
MESH = pl.DeviceIdType.MESH
NT = (((1,), (1,)), ((), ()))
NN = (((1,), (0,)), ((), ()))


def kernel(
    n_ctx,
    n_head,
    table,
    inverse,
    q_ref,
    g_ref,
    kv_ref,
    x_ref,
    kw_ref,
    vw_ref,
    dq_ref,
    x_all,
    w_all,
    rows_all,
    rows_heads,
    kv_all,
    keys,
    values,
    keys_t,
    scores,
    dprobs,
    acc_k,
    acc_v,
    part,
    received,
    own_rows,
    paired,
    outgoing,
    gather_send,
    gather_recv,
    gather_pair_send,
    gather_pair_recv,
    side_send,
    side_recv,
    side_pair_send,
    side_pair_recv,
    x_send,
    x_recv,
    pair_send,
    pair_recv,
    w_send,
    w_recv,
    sum_send,
    sum_recv,
    sum_pair_send,
    sum_pair_recv,
    rows_send,
    rows_recv,
    rows_pair_send,
    rows_pair_recv,
    heads_send,
    heads_recv,
    local_sem,
):
    me = lax.axis_index("ctx")
    head = lax.axis_index("head")
    core = lax.rem(head, 2)
    partner = head + 1 - 2 * core
    side = lax.rem(head // 2, 2)
    across = head + 2 - 4 * side
    ctx_partner = me + 1 - 2 * lax.rem(me, 2)
    strides = n_ctx // 2
    tokens = q_ref.shape[0]
    blk = tokens // 2
    heads = q_ref.shape[1] // HD
    seq = tokens * n_ctx
    blocks = 2 * n_ctx
    cols = x_ref.shape[1] // n_ctx
    half = cols // 2
    feats = kw_ref.shape[0] // n_head
    scale = HD**-0.5
    log2_scale = scale * math.log2(math.e)

    def ctx_peer(d):
        return lax.rem(me + d, n_ctx)

    def ctx_source(d):
        return lax.rem(me + n_ctx - d, n_ctx)

    def head_peer(d):
        return lax.rem(head + d, n_head)

    def ctx_copy(src, dst, send, recv, at, to):
        return pltpu.make_async_remote_copy(
            src_ref=src,
            dst_ref=dst,
            send_sem=send.at[at],
            recv_sem=recv.at[at],
            device_id=(to, head),
            device_id_type=MESH,
        )

    def gather(src, place, sems):
        direct = [
            ctx_copy(src, place(me), sems[0], sems[1], k, ctx_peer(2 * k))
            for k in range(1, strides)
        ]
        passed = [ctx_copy(src, place(me), sems[2], sems[3], 0, ctx_partner)]
        for copy in direct + passed:
            copy.start()
        return direct, passed

    def gather_on(direct, passed, place, sems):
        for k in range(1, strides):
            direct[k - 1].wait()
            piece = place(ctx_source(2 * k))
            copy = ctx_copy(piece, piece, sems[2], sems[3], k, ctx_partner)
            copy.start()
            passed.append(copy)
        for copy in passed:
            copy.wait()

    def head_copy(src, dst, send, recv, at, to):
        return pltpu.make_async_remote_copy(
            src_ref=src,
            dst_ref=dst,
            send_sem=send.at[at],
            recv_sem=recv.at[at],
            device_id=(me, to),
            device_id_type=MESH,
        )

    barrier = pltpu.get_barrier_semaphore()
    for d in range(1, n_ctx):
        pl.semaphore_signal(barrier, inc=1, device_id=(ctx_peer(d), head), device_id_type=MESH)
    for d in range(1, n_head):
        pl.semaphore_signal(barrier, inc=1, device_id=(me, head_peer(d)), device_id_type=MESH)
    pl.semaphore_wait(barrier, n_ctx + n_head - 2)

    own = pl.ds(pl.multiple_of(me * tokens, tokens), tokens)
    def kv_place(source):
        return kv_all.at[pl.ds(2 * source, 2)]

    kv_sems = (gather_send, gather_recv, gather_pair_send, gather_pair_recv)
    kv_direct, kv_passed = gather(kv_ref, kv_place, kv_sems)
    w_copies = []
    for d in range(1, n_head):
        to = head_peer(d)
        for i, ref in enumerate((kw_ref, vw_ref)):
            w_copies.append(
                head_copy(
                    ref.at[pl.ds(pl.multiple_of(to * feats, feats), feats)],
                    w_all.at[:, pl.ds(pl.multiple_of((head * 2 + i) * HD, HD), HD)],
                    w_send,
                    w_recv,
                    2 * d + i,
                    to,
                )
            )
    for copy in w_copies:
        copy.start()
    locals_ = [
        pltpu.make_async_copy(
            x_ref.at[:, pl.ds(pl.multiple_of(me * cols, cols), cols)],
            x_all.at[own],
            local_sem.at[0],
        )
    ]
    own_feats = pl.ds(pl.multiple_of(head * feats, feats), feats)
    for i, ref in enumerate((kw_ref, vw_ref)):
        locals_.append(
            pltpu.make_async_copy(
                ref.at[own_feats],
                w_all.at[:, pl.ds(pl.multiple_of((head * 2 + i) * HD, HD), HD)],
                local_sem.at[1 + i],
            )
        )
    for copy in locals_:
        copy.start()
    kv_all[pl.ds(2 * me, 2)] = kv_ref[...]
    gather_on(kv_direct, kv_passed, kv_place, kv_sems)

    quarter = half // 4
    direct_first = core * half + side * quarter
    x_copies = []
    for d in range(1, n_ctx):
        first = ctx_peer(d) * cols + direct_first
        x_copies.append(
            ctx_copy(
                x_ref.at[:, pl.ds(pl.multiple_of(first, quarter), half - quarter)],
                x_all.at[own, pl.ds(pl.multiple_of(direct_first, quarter), half - quarter)],
                x_send,
                x_recv,
                d,
                ctx_peer(d),
            )
        )
    for copy in x_copies:
        copy.start()

    def sort_block(u, carry):
        from_rows = kv_all[inverse[u]]
        to_rows = pl.ds(pl.multiple_of(u * blk, blk), blk)
        keys[to_rows, :] = from_rows[:, :HD]
        values[to_rows, :] = from_rows[:, HD:]
        keys_t[:, to_rows] = from_rows[:, :HD].T
        return carry

    lax.fori_loop(0, blocks, sort_block, 0)
    acc_k[...] = jnp.zeros_like(acc_k)
    acc_v[...] = jnp.zeros_like(acc_v)

    block_0 = table[2 * me]
    block_1 = table[2 * me + 1]
    top_block = jnp.maximum(block_0, block_1)
    chunk = min(512, seq // 2)
    width = 2 * blk

    first_is_top = jnp.full((width, HD), block_0, jnp.int32) == top_block

    def load(ref, pair):
        halves = []
        for slot in range(2):
            rows = slice(slot * blk, (slot + 1) * blk)
            halves.append(
                jnp.concatenate(
                    [
                        ref[rows, pl.ds(pl.multiple_of((2 * pair + i) * HD, HD), HD)]
                        for i in range(2)
                    ],
                    axis=0,
                ).astype(jnp.float32)
            )
        first, second = halves
        return (
            jnp.where(first_is_top, first, second).astype(jnp.bfloat16),
            jnp.where(first_is_top, second, first).astype(jnp.bfloat16),
        )

    def attend(q, g, block_id, extent, free):
        top = None
        for start in range(0, extent, chunk):
            rows = slice(start, start + chunk)
            s = lax.dot_general(keys[rows, :], q, NT, preferred_element_type=jnp.float32)
            if start + chunk > free:
                key_pos = lax.broadcasted_iota(jnp.int32, (chunk, width), 0)
                row_pos = lax.rem(lax.broadcasted_iota(jnp.int32, (chunk, width), 1), blk)
                s = jnp.where(key_pos - row_pos <= block_id * blk - start, s, -1e30)
            scores[rows, :] = s
            here = jnp.max(s, axis=0, keepdims=True)
            top = here if top is None else jnp.maximum(top, here)
        top = top * log2_scale
        norm = jnp.zeros((1, width), jnp.float32)
        delta = jnp.zeros((1, width), jnp.float32)
        for start in range(0, extent, chunk):
            rows = slice(start, start + chunk)
            prob = jnp.exp2(scores[rows, :] * log2_scale - top)
            dp = lax.dot_general(values[rows, :], g, NT, preferred_element_type=jnp.float32)
            norm = norm + jnp.sum(prob, axis=0, keepdims=True)
            delta = delta + jnp.sum(prob * dp, axis=0, keepdims=True)
            scores[rows, :] = prob
            dprobs[rows, :] = dp
        inv = 1.0 / norm
        delta = delta * inv
        dq_t = jnp.zeros((HD, width), jnp.float32)
        for start in range(0, extent, chunk):
            rows = slice(start, start + chunk)
            prob = scores[rows, :] * inv
            ds = (prob * (dprobs[rows, :] - delta)).astype(jnp.bfloat16)
            pieces = slice(start // blk, (start + chunk) // blk)
            acc_v[pieces] += lax.dot_general(
                prob.astype(jnp.bfloat16), g, NN, preferred_element_type=jnp.float32
            ).reshape(-1, blk, HD)
            acc_k[pieces] += lax.dot_general(
                ds, q, NN, preferred_element_type=jnp.float32
            ).reshape(-1, blk, HD)
            dq_t = dq_t + lax.dot_general(
                keys_t[:, rows], ds, NN, preferred_element_type=jnp.float32
            )
        return jnp.concatenate(
            [dq_t[:, i * blk : (i + 1) * blk].T for i in range(2)], axis=0
        ) * scale

    def head_pair(pair, carry):
        q_top, q_low = load(q_ref, pair)
        g_top, g_low = load(g_ref, pair)
        top_grad = attend(q_top, g_top, top_block, seq, seq // 2)
        low_grad = attend(q_low, g_low, blocks - 1 - top_block, seq // 2, 0)
        for slot, grads in enumerate(
            (
                jnp.where(first_is_top, top_grad, low_grad),
                jnp.where(first_is_top, low_grad, top_grad),
            )
        ):
            for i in range(2):
                dq_ref[
                    slot * blk : (slot + 1) * blk,
                    pl.ds(pl.multiple_of((2 * pair + i) * HD, HD), HD),
                ] = grads[i * blk : (i + 1) * blk].astype(jnp.bfloat16)
        return carry

    lax.fori_loop(0, heads // 2, head_pair, 0)

    def unsort(s, carry):
        to_rows = pl.ds(pl.multiple_of(s * blk, blk), blk)
        part[to_rows, :HD] = (acc_k[table[s]] * scale).astype(jnp.bfloat16)
        part[to_rows, HD:] = acc_v[table[s]].astype(jnp.bfloat16)
        return carry

    lax.fori_loop(0, blocks, unsort, 0)

    pair_sums = []
    for k in range(strides):
        target = lax.rem(ctx_partner + 2 * k, n_ctx)
        to_rows = pl.ds(pl.multiple_of(target * tokens, tokens), tokens)
        pair_sums.append(
            ctx_copy(
                part.at[to_rows], paired.at[k], sum_pair_send, sum_pair_recv, k, ctx_partner
            )
        )
    order = list(range(1, strides)) + [0]
    for k in order:
        pair_sums[k].start()
    def x_piece(d, first, size):
        return x_all.at[
            pl.ds(pl.multiple_of(ctx_source(d) * tokens, tokens), tokens),
            pl.ds(pl.multiple_of(first, quarter), size),
        ]

    side_copies = []
    pair_copies = []
    def forward(d):
        x_copies[d - 1].wait()
        edge = x_piece(d, core * half + side * 3 * quarter, quarter)
        copy = head_copy(edge, edge, side_send, side_recv, d, across)
        copy.start()
        side_copies.append(copy)
        piece = x_piece(d, direct_first, half - quarter)
        copy = head_copy(piece, piece, pair_send, pair_recv, d, partner)
        copy.start()
        pair_copies.append(copy)

    for d in range(1, strides):
        forward(d)
    sums = []
    for k in order:
        pair_sums[k].wait()
        rows = pl.ds(pl.multiple_of(ctx_peer(2 * k) * tokens, tokens), tokens)
        total = part[rows, :].astype(jnp.float32) + paired[k].astype(jnp.float32)
        if k:
            outgoing[k] = total.astype(jnp.bfloat16)
            copy = ctx_copy(
                outgoing.at[k], received.at[k], sum_send, sum_recv, k, ctx_peer(2 * k)
            )
            copy.start()
            sums.append(copy)
    for k in range(1, strides):
        sums[k - 1].wait()
        total = total + received[k].astype(jnp.float32)
    own_rows[...] = total.astype(jnp.bfloat16)

    head_cols = pl.ds(pl.multiple_of(head * 2 * HD, 2 * HD), 2 * HD)
    locals_.append(pltpu.make_async_copy(own_rows, rows_all.at[own], local_sem.at[3]))
    locals_.append(pltpu.make_async_copy(own_rows, rows_heads.at[:, head_cols], local_sem.at[4]))
    for copy in locals_[3:]:
        copy.start()
    def rows_place(source):
        return rows_all.at[pl.ds(pl.multiple_of(source * tokens, tokens), tokens)]

    rows_sems = (rows_send, rows_recv, rows_pair_send, rows_pair_recv)
    rows_direct, rows_passed = gather(own_rows, rows_place, rows_sems)
    rows_copies = []
    for d in range(1, n_head):
        rows_copies.append(
            head_copy(
                own_rows, rows_heads.at[:, head_cols], heads_send, heads_recv, d, head_peer(d)
            )
        )
    for copy in rows_copies:
        copy.start()

    for d in range(strides, n_ctx):
        forward(d)
    gather_on(rows_direct, rows_passed, rows_place, rows_sems)
    for d in range(1, n_ctx):
        side_copies[d - 1].wait()
        piece = x_piece(d, core * half + (1 - side) * 3 * quarter, quarter)
        copy = head_copy(piece, piece, side_pair_send, side_pair_recv, d, partner)
        copy.start()
        pair_copies.append(copy)
    for copy in w_copies + rows_copies + pair_copies + locals_:
        copy.wait()


def local(
    n_ctx,
    n_head,
    layer_input,
    queries,
    saved_keys,
    saved_values,
    grad_output,
    key_weight,
    value_weight,
    block_table,
):
    tokens = queries.shape[0]
    blk = tokens // 2
    seq = tokens * n_ctx
    cols = layer_input.shape[1] // n_ctx
    feats = key_weight.shape[0] // n_head
    table = block_table.reshape(-1)
    slots = jnp.arange(table.shape[0], dtype=jnp.int32)
    inverse = jnp.sum(jnp.where(table[None, :] == slots[:, None], slots[None, :], 0), axis=1)
    saved = jnp.concatenate([saved_keys, saved_values], axis=1).reshape(2, blk, 2 * HD)
    smem = pl.BlockSpec(memory_space=pltpu.SMEM)
    vmem = pl.BlockSpec(memory_space=pltpu.VMEM)
    hbm = pl.BlockSpec(memory_space=pl.ANY)
    bf16 = jnp.bfloat16
    f32 = jnp.float32
    dma = pltpu.SemaphoreType.DMA
    dq, x_all, w_all, rows_all, rows_heads = pl.pallas_call(
        functools.partial(kernel, n_ctx, n_head),
        out_shape=(
            jax.ShapeDtypeStruct(queries.shape, bf16),
            jax.ShapeDtypeStruct((seq, cols), bf16),
            jax.ShapeDtypeStruct((feats, n_head * 2 * HD), bf16),
            jax.ShapeDtypeStruct((seq, 2 * HD), bf16),
            jax.ShapeDtypeStruct((tokens, n_head * 2 * HD), bf16),
        ),
        in_specs=[smem, smem, vmem, vmem, vmem, hbm, hbm, hbm],
        out_specs=(vmem, hbm, hbm, hbm, hbm),
        scratch_shapes=[
            pltpu.VMEM((2 * n_ctx, blk, 2 * HD), bf16),
            pltpu.VMEM((seq, HD), bf16),
            pltpu.VMEM((seq, HD), bf16),
            pltpu.VMEM((HD, seq), bf16),
            pltpu.VMEM((seq, 2 * blk), f32),
            pltpu.VMEM((seq, 2 * blk), f32),
            pltpu.VMEM((2 * n_ctx, blk, HD), f32),
            pltpu.VMEM((2 * n_ctx, blk, HD), f32),
            pltpu.VMEM((seq, 2 * HD), bf16),
            pltpu.VMEM((n_ctx, tokens, 2 * HD), bf16),
            pltpu.VMEM((tokens, 2 * HD), bf16),
            pltpu.VMEM((n_ctx // 2, tokens, 2 * HD), bf16),
            pltpu.VMEM((n_ctx // 2, tokens, 2 * HD), bf16),
            dma((n_ctx,)),
            dma((n_ctx,)),
            dma((n_ctx,)),
            dma((n_ctx,)),
            dma((n_ctx,)),
            dma((n_ctx,)),
            dma((n_ctx,)),
            dma((n_ctx,)),
            dma((n_ctx,)),
            dma((n_ctx,)),
            dma((n_ctx,)),
            dma((n_ctx,)),
            dma((2 * n_head,)),
            dma((2 * n_head,)),
            dma((n_ctx,)),
            dma((n_ctx,)),
            dma((n_ctx,)),
            dma((n_ctx,)),
            dma((n_ctx,)),
            dma((n_ctx,)),
            dma((n_ctx,)),
            dma((n_ctx,)),
            dma((n_head,)),
            dma((n_head,)),
            dma((5,)),
        ],
        compiler_params=pltpu.CompilerParams(
            collective_id=0, has_side_effects=True, vmem_limit_bytes=48 * 1024 * 1024
        ),
    )(table, inverse, queries, grad_output, saved, layer_input, key_weight, value_weight)
    contract = (((0,), (0,)), ((), ()))
    gradients = lax.dot_general(x_all, rows_all, contract, preferred_element_type=f32)
    grad_input = lax.dot_general(rows_heads, w_all, NT, preferred_element_type=f32).astype(bf16)
    return dq, gradients[:, :HD], gradients[:, HD:], grad_input


def solution(mesh):
    both = P("ctx", "head")
    in_specs = (P("ctx", None), both, both, both, both, P(None, "head"), P(None, "head"), P())
    out_specs = (both, both, both, both)
    return jax.shard_map(
        functools.partial(local, mesh.shape["ctx"], mesh.shape["head"]),
        mesh=mesh,
        in_specs=in_specs,
        out_specs=out_specs,
        check_vma=False,
    )
```
